256 devices in a mesh: dp: 64 (over y, z, core), mp: 4 (over x).
Axes of the slice: x: 4, y: 4, z: 8, core: 2. Of those that a mesh axis runs over, the one named last changes fastest.
Arguments:
- grads: float32 [1, 12, 512, 6144], P(None, None, 'dp', 'mp')
- left_stats: float32 [4, 64, 512, 512], P('mp', 'dp'), as said below
- previous_right_statistics: float32 [4, 64, 512, 512], P('mp', 'dp'), as said below
- slot_table: int32 [4, 36], P('mp'), may hold values from 0 to 63, as said below
Outputs:
- update: float32 [1, 12, 512, 6144], P(None, None, 'dp', 'mp')
- new_left: float32 [4, 64, 512, 512], P('mp', 'dp')
- new_right: float32 [4, 64, 512, 512], P('mp', 'dp')
The draws below stay inside these ranges and needn't reach their ends.
Inputs may be any that keep to these rules, and one draw needn't show every extreme that they name: slot_table[g, b] = o + p names place p of owner o; different blocks of one group have different slots, and in every group owner 64 - 1 has all 1 places taken and owner 0 holds place 0. Each left_stats[g, s] is symmetric positive definite. Each previous_right_statistics[g, s] is symmetric positive definite.
All inputs are finite; a program needn't handle non-finite values.
Results may differ from the reference program's by a relative error of at most 0.0015.
Values sent between devices are 32-bit elements; how exact they have to be, the bound alone decides.
No kernel may reach another device: no remote copies, remote signals or barrier semaphores. Data moves between devices by JAX's collectives and lax.ppermute only.
A program may use at most 64 MiB of HBM per device.

```python
import jax
import jax.numpy as jnp
from jax import lax

D = 6144
BLOCK_ORDER = 512
MATS = 1
RB = 12
NBLK = 36
SLOTS = 1
SLOTS_PER_GROUP = 64
N_DP = 64
N_MP = 4


def draw_grads(key, part):
    key = jax.random.fold_in(key, 11)
    key_noise, key_rows, key_cols = jax.random.split(key, 3)
    row_frac = jnp.arange(BLOCK_ORDER, dtype=jnp.float32) / (BLOCK_ORDER - 1)
    rising = (3.0 ** (0.5 * row_frac - 0.25))[:, None]
    noise_part = jnp.clip(jax.random.normal(key_noise, (MATS, RB, BLOCK_ORDER, D), jnp.float32), -4.0, 4.0)
    row_scale = jnp.exp(jax.random.uniform(key_rows, (MATS, RB, BLOCK_ORDER, 1), jnp.float32, -1.15, 1.15)) * rising
    col_scale = jnp.exp(jax.random.uniform(key_cols, (MATS, 1, 1, D), jnp.float32, -1.15, 1.15))
    return 0.1 * row_scale * col_scale * noise_part


def stats_matrix(key):
    key_coupling, diagonal_random_key = jax.random.split(key)
    statistics_shape = (N_MP, SLOTS_PER_GROUP, BLOCK_ORDER, BLOCK_ORDER)
    coupling = jax.random.uniform(key_coupling, statistics_shape, jnp.float32, -1.0 / 30.0, 1.0 / 30.0)
    coupling = 0.5 * (coupling + jnp.swapaxes(coupling, -1, -2))
    diagonal_entries = jnp.exp(jax.random.uniform(diagonal_random_key, (N_MP, SLOTS_PER_GROUP, BLOCK_ORDER), jnp.float32, 0.0, 2.0794415))
    identity = jnp.eye(BLOCK_ORDER, dtype=jnp.float32)
    return coupling * (1.0 - identity) + identity * diagonal_entries[..., None, :]


def draw_left_stats(key, part):
    key = jax.random.fold_in(key, 21)
    return stats_matrix(key)


def draw_previous_right_statistics(key, part):
    key = jax.random.fold_in(key, 22)
    return stats_matrix(key)


def draw_slot_table(key, part):
    key = jax.random.fold_in(key, 31)

    def one_group(group_index):
        group_key = jax.random.fold_in(key, group_index)
        placement_key, key_owner = jax.random.split(group_key)
        position = jax.random.permutation(placement_key, NBLK)
        others = jax.random.permutation(key_owner, N_DP - 2) + 1
        fixed_owners = jnp.array([N_DP - 1, 0], dtype=jnp.int32)
        owners = jnp.concatenate([fixed_owners, others.astype(jnp.int32)])
        return (owners[position % N_DP] * SLOTS + position // N_DP).astype(jnp.int32)
    return jax.vmap(one_group)(jnp.arange(N_MP, dtype=jnp.int32))


def setup_inputs(seed: int = 0) -> dict:
    streams_of = jax.random.split(jax.random.key(seed), 5)
    return {
        "grads": draw_grads(jax.random.fold_in(streams_of[4], 71), 0),
        "left_stats": draw_left_stats(jax.random.fold_in(streams_of[4], 71), 0),
        "previous_right_statistics": draw_previous_right_statistics(jax.random.fold_in(streams_of[4], 71), 0),
        "slot_table": draw_slot_table(jax.random.fold_in(streams_of[4], 71), 0),
    }


BETA = 0.9

def product(left_matrix, right_matrix):
    return jnp.dot(left_matrix, right_matrix, precision=lax.Precision.HIGHEST, preferred_element_type=jnp.float32)

def inverse_root(statistic):
    order_size = statistic.shape[-1]
    identity = jnp.eye(order_size, dtype=jnp.float32)
    normalizer = 2.5 / jnp.sqrt(jnp.sum(statistic * statistic) + 1e-06)
    scaled = normalizer * statistic
    step_one = (5.0 * identity - scaled) * 0.25
    squared = product(step_one, step_one)
    fourth = product(squared, squared)
    second = product(fourth, scaled)
    step_two = (5.0 * identity - second) * 0.25
    return jnp.sqrt(jnp.sqrt(normalizer)) * product(step_one, step_two)

def owner_block(grad_block, left_prev, right_prev):
    outer_rows = lax.dot_general(grad_block, grad_block, (((1,), (1,)), ((), ())), precision=lax.Precision.HIGHEST, preferred_element_type=jnp.float32)
    outer_cols = lax.dot_general(grad_block, grad_block, (((0,), (0,)), ((), ())), precision=lax.Precision.HIGHEST, preferred_element_type=jnp.float32)
    left_now = BETA * left_prev + (1.0 - BETA) * outer_rows
    right_now = BETA * right_prev + (1.0 - BETA) * outer_cols
    result = product(product(inverse_root(left_now), grad_block), inverse_root(right_now))
    return (left_now, right_now, result)

def reference(grads, left_stats, previous_right_statistics, slot_table):
    matrices, row_blocks, block_size, model_width = grads.shape
    owners = N_MP
    column_blocks = model_width // (block_size * owners)
    block_count = matrices * row_blocks * column_blocks
    all_slots = left_stats.shape[1]
    blocks = grads.reshape(matrices, row_blocks, block_size, owners, column_blocks, block_size)
    blocks = blocks.transpose(3, 0, 1, 4, 2, 5).reshape(owners, block_count, block_size, block_size)
    grad_sq = lax.optimization_barrier(jnp.sum(grads * grads, axis=(1, 2, 3)))
    block_ids = jnp.broadcast_to(jnp.arange(block_count, dtype=jnp.int32)[None, :], (owners, block_count))
    group_ids = jnp.broadcast_to(jnp.arange(owners, dtype=jnp.int32)[:, None], (owners, block_count))
    slot_block = jnp.full((owners, all_slots), -1, jnp.int32).at[group_ids, slot_table].set(block_ids)

    def per_slot(flat_index):
        group_index = flat_index // all_slots
        position = flat_index % all_slots
        chosen = slot_block[group_index, position]
        grad_block = blocks[group_index, jnp.maximum(chosen, 0)] * (chosen >= 0).astype(jnp.float32)
        return owner_block(grad_block, left_stats[group_index, position], previous_right_statistics[group_index, position])
    left_new, right_new, preconditioned = lax.map(per_slot, jnp.arange(owners * all_slots, dtype=jnp.int32))
    preconditioned = preconditioned.reshape(owners, all_slots, block_size, block_size)
    slot_sq = lax.optimization_barrier(jnp.sum(preconditioned * preconditioned, axis=(2, 3)))
    layer_of = jnp.where(slot_block >= 0, slot_block // (row_blocks * column_blocks), -1)
    matching = layer_of[:, :, None] == jnp.arange(matrices, dtype=jnp.int32)[None, None, :]
    prec_sq = lax.optimization_barrier(jnp.sum(jnp.where(matching, slot_sq[:, :, None], 0.0), axis=(0, 1)))
    graft_ratio = jnp.sqrt(grad_sq / (prec_sq + 1e-06))
    gathered = preconditioned[group_ids, slot_table]
    layers = block_ids // (row_blocks * column_blocks)
    gathered = gathered * graft_ratio[layers][:, :, None, None]
    update = gathered.reshape(owners, matrices, row_blocks, column_blocks, block_size, block_size)
    update = update.transpose(1, 2, 4, 0, 3, 5).reshape(matrices, row_blocks, block_size, model_width)
    return (update, left_new.reshape(owners, all_slots, block_size, block_size), right_new.reshape(owners, all_slots, block_size, block_size))
```

```python
import jax
import jax.numpy as jnp
from jax import lax
from jax.experimental import pallas as pl
from jax.experimental.pallas import tpu as pltpu
from jax.sharding import PartitionSpec as P

BETA = 0.9
F32 = jnp.float32
BF16 = jnp.bfloat16


def multiply(left, right):
    product = [0.0] * (len(left) + len(right) - 1)
    for i, a in enumerate(left):
        for j, b in enumerate(right):
            product[i + j] += a * b
    return product


def root_coefficients():
    t = [1.25, -0.25]
    fifth = [1.0]
    for _ in range(5):
        fifth = multiply(fifth, t)
    poly = [0.0] * 7
    for i, a in enumerate(t):
        poly[i] += 1.25 * a
    for i, a in enumerate(multiply([0.0, 0.25], fifth)):
        poly[i] -= a
    return poly


C = root_coefficients()


def split(x):
    high = x.astype(BF16)
    return high, (x - high.astype(F32)).astype(BF16)


def dot(a, b, transposed):
    dims = (((1,), (1 if transposed else 0,)), ((), ()))
    return lax.dot_general(a, b, dims, preferred_element_type=F32)


def product(a, b, transposed=False):
    (ah, al), (bh, bl) = a, b
    return dot(ah, bh, transposed) + (dot(ah, bl, transposed) + dot(al, bh, transposed))


def pack_kernel(columns, slots_ref, grads_ref, out_ref, sem):
    size = out_ref.shape[-1]
    blocks = slots_ref.shape[0]
    copies = []
    for b in range(blocks):
        r, c = divmod(b, columns)
        copies.append(
            pltpu.make_async_copy(
                grads_ref.at[r, :, pl.ds(c * size, size)],
                out_ref.at[slots_ref[b]],
                sem.at[b],
            )
        )
    for copy in copies:
        copy.start()
    for copy in copies:
        copy.wait()


def owner_kernel(
    held_ref, grad_sq_ref, block_ref, left_ref, right_ref,
    new_left_ref, new_right_ref, out_ref,
    block, stats, sem, mh, ml, m2, wh, wl, base, piece,
):
    size = block.shape[0]
    per = out_ref.shape[0] // 64
    rows_out = size // 64
    grad_sq = grad_sq_ref[0, 0]
    held = held_ref[0, 0] > 0
    loads = [
        pltpu.make_async_copy(source, target, sem.at[i])
        for i, (source, target) in enumerate(
            [(block_ref, block), (left_ref, stats.at[0]), (right_ref, stats.at[1])]
        )
    ]
    stores = [
        pltpu.make_async_copy(stats.at[i], target, sem.at[3 + i])
        for i, target in enumerate([new_left_ref, new_right_ref])
    ]
    for load in loads:
        load.start()
    lane = lax.broadcasted_iota(jnp.int32, (1, 128), 1)

    def write_sums(prec_sq):
        row = jnp.where(lane == 0, prec_sq, jnp.where(lane == 1, grad_sq, 0.0))
        for d in range(64):
            out_ref[pl.ds(d * per + per - 1, 1), :] = row

    @pl.when(jnp.logical_not(held))
    def _():
        for load in loads:
            load.wait()
        for i in range(2):
            stats[i] = BETA * stats[i]
            stores[i].start()
        write_sums(0.0)
        for store in stores:
            store.wait()

    @pl.when(held)
    def _():
        loads[0].wait()
        g = split(block[...])
        gt = split(block[...].T)
        loads[1].wait()
        stats[0] = BETA * stats[0] + (1.0 - BETA) * product(g, g, True)
        stores[0].start()
        loads[2].wait()
        stats[1] = BETA * stats[1] + (1.0 - BETA) * product(gt, g)
        stores[1].start()
        diagonal = lax.broadcasted_iota(jnp.int32, (size, size), 0) == lax.broadcasted_iota(
            jnp.int32, (size, size), 1
        )
        scale = [2.5 / jnp.sqrt(jnp.sum(stats[i] * stats[i]) + 1e-06) for i in range(2)]
        for i in range(2):
            mh[i], ml[i] = split(scale[i] * stats[i])
        for i in range(2):
            m = (mh[i], ml[i])
            second = product(m, m)
            m2[i] = second
            wh[i], wl[i] = split(second)
        for i in range(2):
            third = product((wh[i], wl[i]), (mh[i], ml[i]))
            m = scale[i] * stats[i]
            second = m2[i]
            base[i] = jnp.where(diagonal, C[0], 0.0) + C[1] * m + (C[2] * second + C[3] * third)
            wh[i], wl[i] = split(third)
            mh[i], ml[i] = split(C[4] * m + (C[5] * second + C[6] * third))
        for i in range(2):
            root = base[i] + product((wh[i], wl[i]), (mh[i], ml[i]))
            wh[i], wl[i] = split(jnp.sqrt(jnp.sqrt(scale[i])) * root)
        u = split(product((wh[0], wl[0]), g))
        piece[...] = product(u, (wh[1], wl[1]))
        result = piece[...]
        write_sums(jnp.sum(result * result))
        for d in range(64):
            for t in range(size // 128):
                out_ref[pl.ds(d * per + rows_out * t, rows_out), :] = piece[
                    pl.ds(d * rows_out, rows_out), pl.ds(128 * t, 128)
                ]
        for store in stores:
            store.wait()


def unpack_kernel(columns, slots_ref, ratio_ref, in_ref, out_ref):
    size = out_ref.shape[-1] // columns
    rows = out_ref.shape[1]
    ratio = ratio_ref[0, 0]
    for b in range(slots_ref.shape[0]):
        r, c = divmod(b, columns)
        slot = slots_ref[b]
        for t in range(size // 128):
            out_ref[r, :, pl.ds(c * size + t * 128, 128)] = (
                in_ref[slot, pl.ds(t * rows, rows), 0, :] * ratio
            )


SMEM = pl.BlockSpec(memory_space=pltpu.SMEM)
VMEM = pl.BlockSpec(memory_space=pltpu.VMEM)
ANY = pl.BlockSpec(memory_space=pl.ANY)


def shards(grads, left_stats, previous_right_statistics, slot_table):
    _, row_blocks, block_rows, local_width = grads.shape
    size = left_stats.shape[-1]
    columns = local_width // size
    owners = lax.axis_size("dp")
    groups = lax.axis_size("mp")
    assigned = slot_table[0]
    local = grads[0]
    outgoing = pl.pallas_call(
        lambda *refs: pack_kernel(columns, *refs),
        out_shape=jax.ShapeDtypeStruct((owners, block_rows, size), F32),
        in_specs=[SMEM, ANY],
        out_specs=ANY,
        scratch_shapes=[pltpu.SemaphoreType.DMA((row_blocks * columns,))],
    )(assigned, local)
    arrived = lax.all_to_all(outgoing, "dp", split_axis=0, concat_axis=0, tiled=True)
    grad_sq = jnp.sum(local * local).reshape(1, 1)
    held = jnp.any(assigned == lax.axis_index("dp")).astype(jnp.int32).reshape(1, 1)
    stat = jax.ShapeDtypeStruct((size, size), F32)
    per = (block_rows * size) // 128 + 1
    pair = (2, size, size)
    left_new, right_new, sent = pl.pallas_call(
        owner_kernel,
        out_shape=(stat, stat, jax.ShapeDtypeStruct((owners * per, 128), F32)),
        in_specs=[SMEM, SMEM, ANY, ANY, ANY],
        out_specs=(ANY, ANY, VMEM),
        scratch_shapes=[
            pltpu.VMEM((size, size), F32),
            pltpu.VMEM(pair, F32),
            pltpu.SemaphoreType.DMA((5,)),
            pltpu.VMEM(pair, BF16),
            pltpu.VMEM(pair, BF16),
            pltpu.VMEM(pair, F32),
            pltpu.VMEM(pair, BF16),
            pltpu.VMEM(pair, BF16),
            pltpu.VMEM(pair, F32),
            pltpu.VMEM((size, size), F32),
        ],
        compiler_params=pltpu.CompilerParams(vmem_limit_bytes=40 << 20),
        cost_estimate=pl.CostEstimate(
            flops=60 * size**3, bytes_accessed=6 * 4 * size**2, transcendentals=0
        ),
    )(
        held,
        grad_sq,
        arrived.reshape(size, size),
        left_stats[0, 0],
        previous_right_statistics[0, 0],
    )
    returned = lax.all_to_all(
        sent.reshape(owners, per, 1, 128), "dp", split_axis=0, concat_axis=0, tiled=True
    )
    sums = jnp.sum(returned[:, per - 1, :, :], axis=0)
    total = sums
    for k in range(1, groups):
        total = total + lax.ppermute(sums, "mp", [(i, (i + k) % groups) for i in range(groups)])
    ratio = jnp.sqrt(total[:, 1:2] / (total[:, 0:1] + 1e-06))
    update = pl.pallas_call(
        lambda *refs: unpack_kernel(columns, *refs),
        out_shape=jax.ShapeDtypeStruct(local.shape, F32),
        in_specs=[SMEM, SMEM, VMEM],
        out_specs=VMEM,
        compiler_params=pltpu.CompilerParams(vmem_limit_bytes=16 << 20),
    )(assigned, ratio, returned)
    return (update[None], left_new[None, None], right_new[None, None])


def solution(mesh):
    return jax.shard_map(
        shards,
        mesh=mesh,
        in_specs=(
            P(None, None, "dp", "mp"),
            P("mp", "dp", None, None),
            P("mp", "dp", None, None),
            P("mp", None),
        ),
        out_specs=(P(None, None, "dp", "mp"), P("mp", "dp", None, None), P("mp", "dp", None, None)),
        check_vma=False,
    )
```

```python
import jax
import jax.numpy as jnp
from jax import lax
from jax.experimental import pallas as pl
from jax.experimental.pallas import tpu as pltpu
from jax.sharding import PartitionSpec as P

BETA = 0.9
F32 = jnp.float32
BF16 = jnp.bfloat16


def multiply(left, right):
    product = [0.0] * (len(left) + len(right) - 1)
    for i, a in enumerate(left):
        for j, b in enumerate(right):
            product[i + j] += a * b
    return product


def root_coefficients():
    t = [1.25, -0.25]
    fifth = [1.0]
    for _ in range(5):
        fifth = multiply(fifth, t)
    poly = [0.0] * 7
    for i, a in enumerate(t):
        poly[i] += 1.25 * a
    for i, a in enumerate(multiply([0.0, 0.25], fifth)):
        poly[i] -= a
    return poly


C = root_coefficients()


ALL = slice(None)


def split(x):
    high = x.astype(BF16)
    return high, (x - high.astype(F32)).astype(BF16)


def dot(a, b, transposed):
    dims = (((1,), (1 if transposed else 0,)), ((), ()))
    return lax.dot_general(a, b, dims, preferred_element_type=F32)


def product(a, b, transposed=False):
    (ah, al), (bh, bl) = a, b
    return dot(ah, bh, transposed) + (dot(ah, bl, transposed) + dot(al, bh, transposed))


def part(pair, rows, cols):
    return pair[0][rows, cols], pair[1][rows, cols]


def pack_kernel(columns, slots_hbm, grads_ref, out_ref, slots_ref, held, sem, slots_sem):
    size = out_ref.shape[-1]
    row_blocks = grads_ref.shape[0]
    loads = [
        pltpu.make_async_copy(grads_ref.at[r], held.at[r], sem.at[r]) for r in range(row_blocks)
    ]
    fetch = pltpu.make_async_copy(slots_hbm, slots_ref, slots_sem)
    fetch.start()
    for load in loads:
        load.start()
    fetch.wait()
    for r in range(row_blocks):
        loads[r].wait()
        for c in range(columns):
            out_ref[slots_ref[r * columns + c]] = held[r, :, pl.ds(c * size, size)]


def owner_kernel(
    held_ref, grad_sq_ref, block_ref, left_ref, right_ref,
    new_left_ref, new_right_ref, out_ref,
    stats, sem, g, gt, ah, al, mh, ml, kh, kl, eye, piece,
):
    size = block_ref.shape[0]
    half = size // 2
    low, high = slice(0, half), slice(half, size)
    previous = [left_ref, right_ref]
    owners = 64
    per = out_ref.shape[0] // owners
    rows_out = size // owners
    grad_sq = grad_sq_ref[0, 0]
    held = held_ref[0, 0] > 0
    stores = [
        pltpu.make_async_copy(stats.at[i], target, sem.at[i])
        for i, target in enumerate([new_left_ref, new_right_ref])
    ]
    lane = lax.broadcasted_iota(jnp.int32, (1, 128), 1)

    def write_sums(prec_sq):
        row = jnp.where(lane == 0, prec_sq, jnp.where(lane == 1, grad_sq, 0.0))
        for d in range(owners):
            out_ref[pl.ds(d * per + per - 1, 1), :] = row

    @pl.when(jnp.logical_not(held))
    def _():
        for i in range(2):
            stats[i] = BETA * previous[i][...]
            stores[i].start()
        write_sums(0.0)
        for store in stores:
            store.wait()

    @pl.when(held)
    def _():
        g[0], g[1] = split(block_ref[...])
        for i in range(2):
            gt[i] = g[i].T
        eye[...] = (
            lax.broadcasted_iota(jnp.int32, (half, half), 0)
            == lax.broadcasted_iota(jnp.int32, (half, half), 1)
        ).astype(F32)
        whole = (g[0], g[1])
        flipped = (gt[0], gt[1])
        scale, scale_sq = [], []
        for i in range(2):
            if i == 0:
                wide = product(whole, part(whole, high, ALL), True)
                corner = product(part(whole, low, ALL), part(whole, low, ALL), True)
            else:
                wide = product(flipped, part(whole, ALL, high))
                corner = product(part(flipped, low, ALL), part(whole, ALL, low))
            total = 0.0
            for rows, cols, outer in (
                (low, low, corner),
                (low, high, wide[low]),
                (high, high, wide[high]),
                (high, low, wide[low].T),
            ):
                now = BETA * previous[i][rows, cols] + (1.0 - BETA) * outer
                stats[i, rows, cols] = now
                total = total + jnp.sum(now * now)
                ah[i, rows, cols], al[i, rows, cols] = split(now)
            stores[i].start()
            scale.append(2.5 / jnp.sqrt(total + 1e-06))
            scale_sq.append(6.25 / (total + 1e-06))

        def put(to_high, to_low, i, rows, cols, value):
            to_high[i, rows, cols], to_low[i, rows, cols] = split(value)

        def mirror(i, *refs):
            for ref in refs:
                ref[i, high, low] = ref[i, low, high].T

        for i in range(2):
            a = (ah[i], al[i])
            wide = product(a, part(a, ALL, high))
            corner = product(part(a, low, ALL), part(a, ALL, low))
            for rows, cols, outer in ((low, low, corner), (low, high, wide[low]), (high, high, wide[high])):
                second = scale_sq[i] * outer
                put(mh, ml, i, rows, cols, second)
                value = (C[5] * scale[i]) * stats[i, rows, cols] + C[6] * second
                if rows == cols:
                    value = value + C[4] * eye[...]
                put(kh, kl, i, rows, cols, value)
            mirror(i, mh, ml, kh, kl)
        for first, constant in ((C[3], C[2]), (C[1], C[0])):
            for i in range(2):
                m, k = (mh[i], ml[i]), (kh[i], kl[i])
                wide = product(m, part(k, ALL, high))
                corner = product(part(m, low, ALL), part(k, ALL, low))
                for rows, cols, outer in ((low, low, corner), (low, high, wide[low]), (high, high, wide[high])):
                    value = (first * scale[i]) * stats[i, rows, cols] + outer
                    if rows == cols:
                        value = value + constant * eye[...]
                    put(kh, kl, i, rows, cols, value)
                mirror(i, kh, kl)
        both = jnp.sqrt(jnp.sqrt(scale[0])) * jnp.sqrt(jnp.sqrt(scale[1]))
        u = split(both * product((kh[0], kl[0]), (g[0], g[1])))
        result = product(u, (kh[1], kl[1]))
        piece[...] = result
        write_sums(jnp.sum(result * result))
        for d in range(owners):
            for t in range(size // 128):
                out_ref[pl.ds(d * per + rows_out * t, rows_out), :] = piece[
                    pl.ds(d * rows_out, rows_out), pl.ds(128 * t, 128)
                ]
        for store in stores:
            store.wait()


def gather_kernel(columns, slots_ref, in_ref, out_ref):
    size = out_ref.shape[-1] // columns
    rows = out_ref.shape[1]
    for b in range(slots_ref.shape[0]):
        r, c = divmod(b, columns)
        slot = slots_ref[b]
        for t in range(size // 128):
            out_ref[r, :, pl.ds(c * size + t * 128, 128)] = in_ref[slot, pl.ds(t * rows, rows), 0, :]


def graft_kernel(*refs):
    *sum_refs, in_ref, out_ref, scaled, sem = refs
    total = sum_refs[0][...]
    for ref in sum_refs[1:]:
        total = total + ref[...]
    ratio = jnp.sqrt(total[:, 1:2] / (total[:, 0:1] + 1e-06))
    copies = []
    for r in range(in_ref.shape[0]):
        scaled[r] = in_ref[r] * ratio
        copies.append(pltpu.make_async_copy(scaled.at[r], out_ref.at[r], sem.at[r]))
        copies[-1].start()
    for copy in copies:
        copy.wait()


SMEM = pl.BlockSpec(memory_space=pltpu.SMEM)
VMEM = pl.BlockSpec(memory_space=pltpu.VMEM)
ANY = pl.BlockSpec(memory_space=pl.ANY)


def shards(grads, left_stats, previous_right_statistics, slot_table):
    _, row_blocks, block_rows, local_width = grads.shape
    size = left_stats.shape[-1]
    columns = local_width // size
    owners = lax.axis_size("dp")
    groups = lax.axis_size("mp")
    assigned = slot_table[0]
    local = grads[0]
    outgoing = pl.pallas_call(
        lambda *refs: pack_kernel(columns, *refs),
        out_shape=jax.ShapeDtypeStruct((owners, block_rows, size), F32),
        in_specs=[ANY, ANY],
        out_specs=VMEM,
        scratch_shapes=[
            pltpu.SMEM(assigned.shape, jnp.int32),
            pltpu.VMEM(local.shape, F32),
            pltpu.SemaphoreType.DMA((row_blocks,)),
            pltpu.SemaphoreType.DMA(()),
        ],
    )(assigned, local)
    arrived = lax.all_to_all(outgoing, "dp", split_axis=0, concat_axis=0, tiled=True)
    grad_sq = jnp.sum(local * local).reshape(1, 1)
    held = jnp.any(assigned == lax.axis_index("dp")).astype(jnp.int32).reshape(1, 1)
    stat = jax.ShapeDtypeStruct((size, size), F32)
    per = (block_rows * size) // 128 + 1
    pair = (2, size, size)
    left_new, right_new, sent = pl.pallas_call(
        owner_kernel,
        out_shape=(stat, stat, jax.ShapeDtypeStruct((owners * per, 128), F32)),
        in_specs=[SMEM, SMEM, VMEM, VMEM, VMEM],
        out_specs=(ANY, ANY, VMEM),
        scratch_shapes=[
            pltpu.VMEM(pair, F32),
            pltpu.SemaphoreType.DMA((2,)),
            *[pltpu.VMEM(pair, BF16)] * 8,
            pltpu.VMEM((size // 2, size // 2), F32),
            pltpu.VMEM((size, size), F32),
        ],
        compiler_params=pltpu.CompilerParams(vmem_limit_bytes=40 << 20),
        cost_estimate=pl.CostEstimate(
            flops=60 * size**3, bytes_accessed=6 * 4 * size**2, transcendentals=0
        ),
    )(
        held,
        grad_sq,
        arrived.reshape(size, size),
        left_stats[0, 0],
        previous_right_statistics[0, 0],
    )
    returned = lax.all_to_all(
        sent.reshape(owners, per, 1, 128), "dp", split_axis=0, concat_axis=0, tiled=True
    )
    sums = jnp.sum(returned[:, per - 1, :, :], axis=0)
    others = [
        lax.ppermute(sums, "mp", [(i, (i + k) % groups) for i in range(groups)])
        for k in range(1, groups)
    ]
    gathered = pl.pallas_call(
        lambda *refs: gather_kernel(columns, *refs),
        out_shape=jax.ShapeDtypeStruct(local.shape, F32),
        in_specs=[SMEM, VMEM],
        out_specs=VMEM,
        compiler_params=pltpu.CompilerParams(vmem_limit_bytes=16 << 20),
        cost_estimate=pl.CostEstimate(flops=0, bytes_accessed=8 << 20, transcendentals=0),
    )(assigned, returned)
    update = pl.pallas_call(
        graft_kernel,
        out_shape=jax.ShapeDtypeStruct(local.shape, F32),
        in_specs=[VMEM] * (groups + 1),
        out_specs=ANY,
        scratch_shapes=[
            pltpu.VMEM(local.shape, F32),
            pltpu.SemaphoreType.DMA((row_blocks,)),
        ],
        compiler_params=pltpu.CompilerParams(vmem_limit_bytes=16 << 20),
    )(sums, *others, gathered)
    return (update[None], left_new[None, None], right_new[None, None])


def solution(mesh):
    return jax.shard_map(
        shards,
        mesh=mesh,
        in_specs=(
            P(None, None, "dp", "mp"),
            P("mp", "dp", None, None),
            P("mp", "dp", None, None),
            P("mp", None),
        ),
        out_specs=(P(None, None, "dp", "mp"), P("mp", "dp", None, None), P("mp", "dp", None, None)),
        check_vma=False,
    )
```

```python
import jax
import jax.numpy as jnp
import numpy as np
from jax import lax
from jax.experimental import pallas as pl
from jax.experimental.pallas import tpu as pltpu
from jax.sharding import PartitionSpec as P

BETA = 0.9
F32 = jnp.float32
BF16 = jnp.bfloat16


poly = np.polynomial.polynomial


def root_plan(first, second, third):
    t = np.array([1.25, -0.25])
    p = poly.polysub(1.25 * t, poly.polymul([0.0, 0.25], poly.polypow(t, 5)))
    d = np.array([first * second, -(first + second), 1.0])
    e, r = poly.polydiv(p, d)
    q = poly.polyval(third, e)
    e = poly.polysub(e, [q])
    f, b = poly.polydiv(e, d)
    s = poly.polyval(third, f)
    f = poly.polysub(f, [s])
    floats = [[float(x) for x in values] for values in (d, r, f, b)]
    return (*floats, float(q), float(s))


D, R, F, B, Q, S = root_plan(0.167, 2.333, 1.25)
BASE_M, BASE_I = Q * D[1] + R[1], Q * D[0] + R[0]
E_BASE = S / Q
E_M, E_I = S * D[1] + B[1] - E_BASE * BASE_M, S * D[0] + B[0] - E_BASE * BASE_I
ALL = slice(None)


def split(x):
    high = x.astype(BF16)
    return high, (x - high.astype(F32)).astype(BF16)


def dot(a, b, transposed):
    dims = (((1,), (1 if transposed else 0,)), ((), ()))
    return lax.dot_general(a, b, dims, preferred_element_type=F32)


def product(a, b, transposed=False):
    (ah, al), (bh, bl) = a, b
    return dot(ah, bh, transposed) + (dot(ah, bl, transposed) + dot(al, bh, transposed))


def part(pair, rows, cols):
    return pair[0][rows, cols], pair[1][rows, cols]


def pack_kernel(columns, slots_hbm, grads_ref, out_ref, slots_ref, held, sem, slots_sem):
    size = out_ref.shape[-1]
    row_blocks = grads_ref.shape[0]
    loads = [
        pltpu.make_async_copy(grads_ref.at[r], held.at[r], sem.at[r]) for r in range(row_blocks)
    ]
    fetch = pltpu.make_async_copy(slots_hbm, slots_ref, slots_sem)
    fetch.start()
    for load in loads:
        load.start()
    fetch.wait()
    for r in range(row_blocks):
        loads[r].wait()
        for c in range(columns):
            out_ref[slots_ref[r * columns + c]] = held[r, :, pl.ds(c * size, size)]


def owner_kernel(
    held_ref, grad_sq_ref, block_ref, left_ref, right_ref,
    new_left_ref, new_right_ref, out_ref,
    stats, sem, g, gt, ah, al, dm, fm, em, kh, kl, base, eye, piece,
):
    size = block_ref.shape[0]
    half = size // 2
    low, high = slice(0, half), slice(half, size)
    previous = [left_ref, right_ref]
    owners = 64
    per = out_ref.shape[0] // owners
    rows_out = size // owners
    grad_sq = grad_sq_ref[0, 0]
    held = held_ref[0, 0] > 0
    stores = [
        pltpu.make_async_copy(stats.at[i], target, sem.at[i])
        for i, target in enumerate([new_left_ref, new_right_ref])
    ]
    lane = lax.broadcasted_iota(jnp.int32, (1, 128), 1)

    def write_sums(prec_sq):
        row = jnp.where(lane == 0, prec_sq, jnp.where(lane == 1, grad_sq, 0.0))
        for d in range(owners):
            out_ref[pl.ds(d * per + per - 1, 1), :] = row

    @pl.when(jnp.logical_not(held))
    def _():
        for i in range(2):
            stats[i] = BETA * previous[i][...]
            stores[i].start()
        write_sums(0.0)
        for store in stores:
            store.wait()

    @pl.when(held)
    def _():
        g[0], g[1] = split(block_ref[...])
        for i in range(2):
            gt[i] = g[i].T
        eye[...] = (
            lax.broadcasted_iota(jnp.int32, (half, half), 0)
            == lax.broadcasted_iota(jnp.int32, (half, half), 1)
        ).astype(F32)
        whole = (g[0], g[1])
        flipped = (gt[0], gt[1])
        scale, scale_sq = [], []
        for i in range(2):
            if i == 0:
                wide = product(whole, part(whole, high, ALL), True)
                corner = product(part(whole, low, ALL), part(whole, low, ALL), True)
            else:
                wide = product(flipped, part(whole, ALL, high))
                corner = product(part(flipped, low, ALL), part(whole, ALL, low))
            total = 0.0
            for rows, cols, outer in (
                (low, low, corner),
                (low, high, wide[low]),
                (high, high, wide[high]),
                (high, low, wide[low].T),
            ):
                now = BETA * previous[i][rows, cols] + (1.0 - BETA) * outer
                stats[i, rows, cols] = now
                total = total + jnp.sum(now * now)
                ah[i, rows, cols], al[i, rows, cols] = split(now)
            stores[i].start()
            scale.append(2.5 / jnp.sqrt(total + 1e-06))
            scale_sq.append(6.25 / (total + 1e-06))

        def quarters(corner, wide):
            return (low, low, corner), (low, high, wide[low]), (high, high, wide[high])

        def mirror(i, *refs):
            for ref in refs:
                ref[i, high, low] = ref[i, low, high].T

        for i in range(2):
            a = (ah[i], al[i])
            wide = product(a, part(a, ALL, high))
            corner = product(part(a, low, ALL), part(a, ALL, low))
            for rows, cols, outer in quarters(corner, wide):
                m = scale[i] * stats[i, rows, cols]
                second = scale_sq[i] * outer
                dv = second + D[1] * m
                fv = F[2] * second + F[1] * m
                bv = Q * second + BASE_M * m
                if rows == cols:
                    dv = dv + D[0] * eye[...]
                    fv = fv + F[0] * eye[...]
                    bv = bv + BASE_I * eye[...]
                dm[i, rows, cols] = dv.astype(BF16)
                fm[i, rows, cols] = fv.astype(BF16)
                base[i, rows, cols] = bv
            mirror(i, dm, fm)
        for i in range(2):
            wide = dot(dm[i], fm[i, :, high], False)
            corner = dot(dm[i, low, :], fm[i, :, low], False)
            for rows, cols, outer in quarters(corner, wide):
                ev = outer + E_BASE * base[i, rows, cols] + (E_M * scale[i]) * stats[i, rows, cols]
                if rows == cols:
                    ev = ev + E_I * eye[...]
                em[i, rows, cols] = ev.astype(BF16)
            mirror(i, em)
        for i in range(2):
            wide = dot(dm[i], em[i, :, high], False)
            corner = dot(dm[i, low, :], em[i, :, low], False)
            for rows, cols, outer in quarters(corner, wide):
                kh[i, rows, cols], kl[i, rows, cols] = split(outer + base[i, rows, cols])
            mirror(i, kh, kl)
        both = jnp.sqrt(jnp.sqrt(scale[0])) * jnp.sqrt(jnp.sqrt(scale[1]))
        u = split(both * product((kh[0], kl[0]), (g[0], g[1])))
        result = product(u, (kh[1], kl[1]))
        piece[...] = result
        write_sums(jnp.sum(result * result))
        for d in range(owners):
            for t in range(size // 128):
                out_ref[pl.ds(d * per + rows_out * t, rows_out), :] = piece[
                    pl.ds(d * rows_out, rows_out), pl.ds(128 * t, 128)
                ]
        for store in stores:
            store.wait()


def gather_kernel(columns, slots_ref, in_ref, out_ref):
    size = out_ref.shape[-1] // columns
    rows = out_ref.shape[1]
    for b in range(slots_ref.shape[0]):
        r, c = divmod(b, columns)
        slot = slots_ref[b]
        for t in range(size // 128):
            out_ref[r, :, pl.ds(c * size + t * 128, 128)] = in_ref[slot, pl.ds(t * rows, rows), 0, :]


def graft_kernel(*refs):
    *sum_refs, in_ref, out_ref, scaled, sem = refs
    total = sum_refs[0][...]
    for ref in sum_refs[1:]:
        total = total + ref[...]
    ratio = jnp.sqrt(total[:, 1:2] / (total[:, 0:1] + 1e-06))
    copies = []
    for r in range(in_ref.shape[0]):
        scaled[r] = in_ref[r] * ratio
        copies.append(pltpu.make_async_copy(scaled.at[r], out_ref.at[r], sem.at[r]))
        copies[-1].start()
    for copy in copies:
        copy.wait()


SMEM = pl.BlockSpec(memory_space=pltpu.SMEM)
VMEM = pl.BlockSpec(memory_space=pltpu.VMEM)
ANY = pl.BlockSpec(memory_space=pl.ANY)


def shards(grads, left_stats, previous_right_statistics, slot_table):
    _, row_blocks, block_rows, local_width = grads.shape
    size = left_stats.shape[-1]
    columns = local_width // size
    owners = lax.axis_size("dp")
    groups = lax.axis_size("mp")
    assigned = slot_table[0]
    local = grads[0]
    outgoing = pl.pallas_call(
        lambda *refs: pack_kernel(columns, *refs),
        out_shape=jax.ShapeDtypeStruct((owners, block_rows, size), F32),
        in_specs=[ANY, ANY],
        out_specs=VMEM,
        scratch_shapes=[
            pltpu.SMEM(assigned.shape, jnp.int32),
            pltpu.VMEM(local.shape, F32),
            pltpu.SemaphoreType.DMA((row_blocks,)),
            pltpu.SemaphoreType.DMA(()),
        ],
    )(assigned, local)
    arrived = lax.all_to_all(outgoing, "dp", split_axis=0, concat_axis=0, tiled=True)
    grad_sq = jnp.sum(local * local).reshape(1, 1)
    held = jnp.any(assigned == lax.axis_index("dp")).astype(jnp.int32).reshape(1, 1)
    stat = jax.ShapeDtypeStruct((size, size), F32)
    per = (block_rows * size) // 128 + 1
    pair = (2, size, size)
    left_new, right_new, sent = pl.pallas_call(
        owner_kernel,
        out_shape=(stat, stat, jax.ShapeDtypeStruct((owners * per, 128), F32)),
        in_specs=[SMEM, SMEM, VMEM, VMEM, VMEM],
        out_specs=(ANY, ANY, VMEM),
        scratch_shapes=[
            pltpu.VMEM(pair, F32),
            pltpu.SemaphoreType.DMA((2,)),
            *[pltpu.VMEM(pair, BF16)] * 9,
            pltpu.VMEM(pair, F32),
            pltpu.VMEM((size // 2, size // 2), F32),
            pltpu.VMEM((size, size), F32),
        ],
        compiler_params=pltpu.CompilerParams(vmem_limit_bytes=40 << 20),
        cost_estimate=pl.CostEstimate(
            flops=60 * size**3, bytes_accessed=6 * 4 * size**2, transcendentals=0
        ),
    )(
        held,
        grad_sq,
        arrived.reshape(size, size),
        left_stats[0, 0],
        previous_right_statistics[0, 0],
    )
    returned = lax.all_to_all(
        sent.reshape(owners, per, 1, 128), "dp", split_axis=0, concat_axis=0, tiled=True
    )
    sums = jnp.sum(returned[:, per - 1, :, :], axis=0)
    others = [
        lax.ppermute(sums, "mp", [(i, (i + k) % groups) for i in range(groups)])
        for k in range(1, groups)
    ]
    gathered = pl.pallas_call(
        lambda *refs: gather_kernel(columns, *refs),
        out_shape=jax.ShapeDtypeStruct(local.shape, F32),
        in_specs=[SMEM, VMEM],
        out_specs=VMEM,
        compiler_params=pltpu.CompilerParams(vmem_limit_bytes=16 << 20),
        cost_estimate=pl.CostEstimate(flops=0, bytes_accessed=8 << 20, transcendentals=0),
    )(assigned, returned)
    update = pl.pallas_call(
        graft_kernel,
        out_shape=jax.ShapeDtypeStruct(local.shape, F32),
        in_specs=[VMEM] * (groups + 1),
        out_specs=ANY,
        scratch_shapes=[
            pltpu.VMEM(local.shape, F32),
            pltpu.SemaphoreType.DMA((row_blocks,)),
        ],
        compiler_params=pltpu.CompilerParams(vmem_limit_bytes=16 << 20),
    )(sums, *others, gathered)
    return (update[None], left_new[None, None], right_new[None, None])


def solution(mesh):
    return jax.shard_map(
        shards,
        mesh=mesh,
        in_specs=(
            P(None, None, "dp", "mp"),
            P("mp", "dp", None, None),
            P("mp", "dp", None, None),
            P("mp", None),
        ),
        out_specs=(P(None, None, "dp", "mp"), P("mp", "dp", None, None), P("mp", "dp", None, None)),
        check_vma=False,
    )
```

```python
import jax
import jax.numpy as jnp
import numpy as np
from jax import lax
from jax.experimental import pallas as pl
from jax.experimental.pallas import tpu as pltpu
from jax.sharding import PartitionSpec as P

BETA = 0.9
F32 = jnp.float32
BF16 = jnp.bfloat16


poly = np.polynomial.polynomial


def root_plan(first, second, third):
    t = np.array([1.25, -0.25])
    p = poly.polysub(1.25 * t, poly.polymul([0.0, 0.25], poly.polypow(t, 5)))
    d = np.array([first * second, -(first + second), 1.0])
    e, r = poly.polydiv(p, d)
    q = poly.polyval(third, e)
    e = poly.polysub(e, [q])
    f, b = poly.polydiv(e, d)
    s = poly.polyval(third, f)
    f = poly.polysub(f, [s])
    floats = [[float(x) for x in values] for values in (d, r, f, b)]
    return (*floats, float(q), float(s))


D, R, F, B, Q, S = root_plan(0.167, 2.333, 1.25)
BASE_M, BASE_I = Q * D[1] + R[1], Q * D[0] + R[0]
E_BASE = S / Q
E_M, E_I = S * D[1] + B[1] - E_BASE * BASE_M, S * D[0] + B[0] - E_BASE * BASE_I
ALL = slice(None)


def split(x):
    high = x.astype(BF16)
    return high, (x - high.astype(F32)).astype(BF16)


def dot(a, b, transposed):
    dims = (((1,), (1 if transposed else 0,)), ((), ()))
    return lax.dot_general(a, b, dims, preferred_element_type=F32)


def product(a, b, transposed=False):
    (ah, al), (bh, bl) = a, b
    return dot(ah, bh, transposed) + (dot(ah, bl, transposed) + dot(al, bh, transposed))


def part(pair, rows, cols):
    return pair[0][rows, cols], pair[1][rows, cols]


def pack_kernel(columns, slots_hbm, grads_ref, out_ref, slots_ref, held, sem, slots_sem):
    size = out_ref.shape[-1]
    row_blocks = grads_ref.shape[0]
    loads = [
        pltpu.make_async_copy(grads_ref.at[r], held.at[r], sem.at[r]) for r in range(row_blocks)
    ]
    fetch = pltpu.make_async_copy(slots_hbm, slots_ref, slots_sem)
    fetch.start()
    for load in loads:
        load.start()
    fetch.wait()
    for r in range(row_blocks):
        loads[r].wait()
        for c in range(columns):
            out_ref[slots_ref[r * columns + c]] = held[r, :, pl.ds(c * size, size)]


def owner_kernel(
    held_ref, grad_sq_ref, block_ref, left_ref, right_ref,
    new_left_ref, new_right_ref, out_ref,
    stats, sem, g, gt, ah, al, dm, fm, em, kh, kl, base, eye,
):
    size = block_ref.shape[0]
    half = size // 2
    low, high = slice(0, half), slice(half, size)
    previous = [left_ref, right_ref]
    owners = 64
    per = out_ref.shape[0] // owners
    rows_out = size // owners
    grad_sq = grad_sq_ref[0, 0]
    held = held_ref[0, 0] > 0
    stores = [
        pltpu.make_async_copy(stats.at[i], target, sem.at[i])
        for i, target in enumerate([new_left_ref, new_right_ref])
    ]
    lane = lax.broadcasted_iota(jnp.int32, (1, 128), 1)

    def write_sums(prec_sq):
        row = jnp.where(lane == 0, prec_sq, jnp.where(lane == 1, grad_sq, 0.0))
        for d in range(owners):
            out_ref[pl.ds(d * per + per - 1, 1), :] = row

    @pl.when(jnp.logical_not(held))
    def _():
        for i in range(2):
            stats[i] = BETA * previous[i][...]
            stores[i].start()
        write_sums(0.0)
        for store in stores:
            store.wait()

    @pl.when(held)
    def _():
        g[0], g[1] = split(block_ref[...])
        for i in range(2):
            gt[i] = g[i].T
        eye[...] = (
            lax.broadcasted_iota(jnp.int32, (half, half), 0)
            == lax.broadcasted_iota(jnp.int32, (half, half), 1)
        ).astype(F32)
        whole = (g[0], g[1])
        flipped = (gt[0], gt[1])
        scale, scale_sq = [], []
        for i in range(2):
            if i == 0:
                wide = product(whole, part(whole, high, ALL), True)
                corner = product(part(whole, low, ALL), part(whole, low, ALL), True)
            else:
                wide = product(flipped, part(whole, ALL, high))
                corner = product(part(flipped, low, ALL), part(whole, ALL, low))
            total = 0.0
            for rows, cols, outer in (
                (low, low, corner),
                (low, high, wide[low]),
                (high, high, wide[high]),
                (high, low, wide[low].T),
            ):
                now = BETA * previous[i][rows, cols] + (1.0 - BETA) * outer
                stats[i, rows, cols] = now
                total = total + jnp.sum(now * now)
                ah[i, rows, cols], al[i, rows, cols] = split(now)
            stores[i].start()
            scale.append(2.5 / jnp.sqrt(total + 1e-06))
            scale_sq.append(6.25 / (total + 1e-06))

        def quarters(corner, wide):
            return (low, low, corner), (low, high, wide[low]), (high, high, wide[high])

        def mirror(i, *refs):
            for ref in refs:
                ref[i, high, low] = ref[i, low, high].T

        for i in range(2):
            a = (ah[i], al[i])
            wide = product(a, part(a, ALL, high))
            corner = product(part(a, low, ALL), part(a, ALL, low))
            for rows, cols, outer in quarters(corner, wide):
                m = scale[i] * stats[i, rows, cols]
                second = jnp.where(scale_sq[i] > 0.0, scale_sq[i] * outer, 0.0)
                dv = second + D[1] * m
                fv = F[2] * second + F[1] * m
                bv = Q * second + BASE_M * m
                if rows == cols:
                    dv = dv + D[0] * eye[...]
                    fv = fv + F[0] * eye[...]
                    bv = bv + BASE_I * eye[...]
                dm[i, rows, cols] = dv.astype(BF16)
                fm[i, rows, cols] = fv.astype(BF16)
                base[i, rows, cols] = bv
            mirror(i, dm, fm)
        for i in range(2):
            wide = dot(dm[i], fm[i, :, high], False)
            corner = dot(dm[i, low, :], fm[i, :, low], False)
            for rows, cols, outer in quarters(corner, wide):
                ev = outer + E_BASE * base[i, rows, cols] + (E_M * scale[i]) * stats[i, rows, cols]
                if rows == cols:
                    ev = ev + E_I * eye[...]
                em[i, rows, cols] = ev.astype(BF16)
            mirror(i, em)
        for i in range(2):
            wide = dot(dm[i], em[i, :, high], False)
            corner = dot(dm[i, low, :], em[i, :, low], False)
            for rows, cols, outer in quarters(corner, wide):
                kh[i, rows, cols], kl[i, rows, cols] = split(outer + base[i, rows, cols])
            mirror(i, kh, kl)
        both = jnp.sqrt(jnp.sqrt(scale[0])) * jnp.sqrt(jnp.sqrt(scale[1]))
        u = split(both * product((kh[0], kl[0]), (g[0], g[1])))
        total = 0.0
        for t in range(2):
            cols = (low, high)[t]
            result = product(u, part((kh[1], kl[1]), ALL, cols))
            total = total + jnp.sum(result * result)
            for d in range(owners):
                for j in range(2):
                    out_ref[pl.ds(d * per + rows_out * (2 * t + j), rows_out), :] = result[
                        d * rows_out : (d + 1) * rows_out, 128 * j : 128 * (j + 1)
                    ]
        write_sums(total)
        for store in stores:
            store.wait()


def gather_kernel(columns, slots_ref, in_ref, out_ref):
    size = out_ref.shape[-1] // columns
    rows = out_ref.shape[1]
    for b in range(slots_ref.shape[0]):
        r, c = divmod(b, columns)
        slot = slots_ref[b]
        for t in range(size // 128):
            out_ref[r, :, pl.ds(c * size + t * 128, 128)] = in_ref[slot, pl.ds(t * rows, rows), 0, :]


def graft_kernel(*refs):
    *sum_refs, in_ref, out_ref, scaled, sem = refs
    total = sum_refs[0][...]
    for ref in sum_refs[1:]:
        total = total + ref[...]
    ratio = jnp.sqrt(total[:, 1:2] / (total[:, 0:1] + 1e-06))
    copies = []
    for r in range(in_ref.shape[0]):
        scaled[r] = in_ref[r] * ratio
        copies.append(pltpu.make_async_copy(scaled.at[r], out_ref.at[r], sem.at[r]))
        copies[-1].start()
    for copy in copies:
        copy.wait()


SMEM = pl.BlockSpec(memory_space=pltpu.SMEM)
VMEM = pl.BlockSpec(memory_space=pltpu.VMEM)
ANY = pl.BlockSpec(memory_space=pl.ANY)


def shards(grads, left_stats, previous_right_statistics, slot_table):
    _, row_blocks, block_rows, local_width = grads.shape
    size = left_stats.shape[-1]
    columns = local_width // size
    owners = lax.axis_size("dp")
    groups = lax.axis_size("mp")
    assigned = slot_table[0]
    local = grads[0]
    outgoing = pl.pallas_call(
        lambda *refs: pack_kernel(columns, *refs),
        out_shape=jax.ShapeDtypeStruct((owners, block_rows, size), F32),
        in_specs=[ANY, ANY],
        out_specs=VMEM,
        scratch_shapes=[
            pltpu.SMEM(assigned.shape, jnp.int32),
            pltpu.VMEM(local.shape, F32),
            pltpu.SemaphoreType.DMA((row_blocks,)),
            pltpu.SemaphoreType.DMA(()),
        ],
    )(assigned, local)
    arrived = lax.all_to_all(outgoing, "dp", split_axis=0, concat_axis=0, tiled=True)
    grad_sq = jnp.sum(local * local).reshape(1, 1)
    held = jnp.any(assigned == lax.axis_index("dp")).astype(jnp.int32).reshape(1, 1)
    stat = jax.ShapeDtypeStruct((size, size), F32)
    per = (block_rows * size) // 128 + 1
    pair = (2, size, size)
    left_new, right_new, sent = pl.pallas_call(
        owner_kernel,
        out_shape=(stat, stat, jax.ShapeDtypeStruct((owners * per, 128), F32)),
        in_specs=[SMEM, SMEM, VMEM, VMEM, VMEM],
        out_specs=(ANY, ANY, VMEM),
        scratch_shapes=[
            pltpu.VMEM(pair, F32),
            pltpu.SemaphoreType.DMA((2,)),
            *[pltpu.VMEM(pair, BF16)] * 9,
            pltpu.VMEM(pair, F32),
            pltpu.VMEM((size // 2, size // 2), F32),
        ],
        compiler_params=pltpu.CompilerParams(vmem_limit_bytes=40 << 20),
        cost_estimate=pl.CostEstimate(
            flops=60 * size**3, bytes_accessed=6 * 4 * size**2, transcendentals=0
        ),
    )(
        held,
        grad_sq,
        arrived.reshape(size, size),
        left_stats[0, 0],
        previous_right_statistics[0, 0],
    )
    returned = lax.all_to_all(
        sent.reshape(owners, per, 1, 128), "dp", split_axis=0, concat_axis=0, tiled=True
    )
    sums = jnp.sum(returned[:, per - 1, :, :], axis=0)
    others = [
        lax.ppermute(sums, "mp", [(i, (i + k) % groups) for i in range(groups)])
        for k in range(groups - 1, 0, -1)
    ]
    gathered = pl.pallas_call(
        lambda *refs: gather_kernel(columns, *refs),
        out_shape=jax.ShapeDtypeStruct(local.shape, F32),
        in_specs=[SMEM, VMEM],
        out_specs=VMEM,
        compiler_params=pltpu.CompilerParams(vmem_limit_bytes=16 << 20),
        cost_estimate=pl.CostEstimate(flops=0, bytes_accessed=8 << 20, transcendentals=0),
    )(assigned, returned)
    update = pl.pallas_call(
        graft_kernel,
        out_shape=jax.ShapeDtypeStruct(local.shape, F32),
        in_specs=[VMEM] * (groups + 1),
        out_specs=ANY,
        scratch_shapes=[
            pltpu.VMEM(local.shape, F32),
            pltpu.SemaphoreType.DMA((row_blocks,)),
        ],
        compiler_params=pltpu.CompilerParams(vmem_limit_bytes=16 << 20),
    )(sums, *others, gathered)
    return (update[None], left_new[None, None], right_new[None, None])


def solution(mesh):
    return jax.shard_map(
        shards,
        mesh=mesh,
        in_specs=(
            P(None, None, "dp", "mp"),
            P("mp", "dp", None, None),
            P("mp", "dp", None, None),
            P("mp", None),
        ),
        out_specs=(P(None, None, "dp", "mp"), P("mp", "dp", None, None), P("mp", "dp", None, None)),
        check_vma=False,
    )
```

```python
import jax
import jax.numpy as jnp
import numpy as np
from jax import lax
from jax.experimental import pallas as pl
from jax.experimental.pallas import tpu as pltpu
from jax.sharding import PartitionSpec as P

BETA = 0.9
F32 = jnp.float32
BF16 = jnp.bfloat16


poly = np.polynomial.polynomial


def root_plan(first, second, third):
    t = np.array([1.25, -0.25])
    p = poly.polysub(1.25 * t, poly.polymul([0.0, 0.25], poly.polypow(t, 5)))
    d = np.array([first * second, -(first + second), 1.0])
    e, r = poly.polydiv(p, d)
    q = poly.polyval(third, e)
    e = poly.polysub(e, [q])
    f, b = poly.polydiv(e, d)
    s = poly.polyval(third, f)
    f = poly.polysub(f, [s])
    floats = [[float(x) for x in values] for values in (d, r, f, b)]
    return (*floats, float(q), float(s))


D, R, F, B, Q, S = root_plan(0.167, 2.333, 1.25)
BASE_M, BASE_I = Q * D[1] + R[1], Q * D[0] + R[0]
E_BASE = S / Q
E_M, E_I = S * D[1] + B[1] - E_BASE * BASE_M, S * D[0] + B[0] - E_BASE * BASE_I
ALL = slice(None)


def split(x):
    high = x.astype(BF16)
    return high, (x - high.astype(F32)).astype(BF16)


def dot(a, b, transposed):
    dims = (((1,), (1 if transposed else 0,)), ((), ()))
    return lax.dot_general(a, b, dims, preferred_element_type=F32)


def product(a, b, transposed=False):
    (ah, al), (bh, bl) = a, b
    return dot(ah, bh, transposed) + (dot(ah, bl, transposed) + dot(al, bh, transposed))


def square(a, b, low, high, transposed=False):
    (ah, _), (bh, bl) = a, b
    wide = dot(ah, bh[high, :] if transposed else bh[:, high], transposed)
    corner = dot(ah[low], bh[low, :] if transposed else bh[:, low], transposed)
    cross = dot(ah, bl, transposed)
    return (
        corner + (cross[low, low] + cross[low, low].T),
        wide[low] + (cross[low, high] + cross[high, low].T),
        wide[high] + (cross[high, high] + cross[high, high].T),
    )


def part(pair, rows, cols):
    return pair[0][rows, cols], pair[1][rows, cols]


def pack_kernel(columns, slots_hbm, grads_ref, out_ref, slots_ref, held, sem, slots_sem):
    size = out_ref.shape[-1]
    row_blocks = grads_ref.shape[0]
    loads = [
        pltpu.make_async_copy(grads_ref.at[r], held.at[r], sem.at[r]) for r in range(row_blocks)
    ]
    fetch = pltpu.make_async_copy(slots_hbm, slots_ref, slots_sem)
    fetch.start()
    for load in loads:
        load.start()
    fetch.wait()
    for r in range(row_blocks):
        loads[r].wait()
        for c in range(columns):
            out_ref[slots_ref[r * columns + c]] = held[r, :, pl.ds(c * size, size)]


def owner_kernel(
    held_ref, grad_sq_ref, block_ref, left_ref, right_ref,
    new_left_ref, new_right_ref, out_ref,
    stats, sem, g, gt, ah, al, dm, fm, em, kh, kl, base, eye,
):
    size = block_ref.shape[0]
    half = size // 2
    low, high = slice(0, half), slice(half, size)
    previous = [left_ref, right_ref]
    owners = 64
    per = out_ref.shape[0] // owners
    rows_out = size // owners
    grad_sq = grad_sq_ref[0, 0]
    held = held_ref[0, 0] > 0
    stores = [
        pltpu.make_async_copy(stats.at[i], target, sem.at[i])
        for i, target in enumerate([new_left_ref, new_right_ref])
    ]
    lane = lax.broadcasted_iota(jnp.int32, (1, 128), 1)

    def write_sums(prec_sq):
        row = jnp.where(lane == 0, prec_sq, jnp.where(lane == 1, grad_sq, 0.0))
        for d in range(owners):
            out_ref[pl.ds(d * per + per - 1, 1), :] = row

    @pl.when(jnp.logical_not(held))
    def _():
        for i in range(2):
            stats[i] = BETA * previous[i][...]
            stores[i].start()
        write_sums(0.0)
        for store in stores:
            store.wait()

    @pl.when(held)
    def _():
        g[0], g[1] = split(block_ref[...])
        for i in range(2):
            gt[i] = g[i].T
        eye[...] = (
            lax.broadcasted_iota(jnp.int32, (half, half), 0)
            == lax.broadcasted_iota(jnp.int32, (half, half), 1)
        ).astype(F32)
        whole = (g[0], g[1])
        flipped = (gt[0], gt[1])
        scale, scale_sq = [], []
        for i in range(2):
            if i == 0:
                q00, q01, q11 = square(whole, whole, low, high, True)
            else:
                q00, q01, q11 = square(flipped, whole, low, high)
            total = 0.0
            for rows, cols, outer in (
                (low, low, q00),
                (low, high, q01),
                (high, high, q11),
                (high, low, q01.T),
            ):
                now = BETA * previous[i][rows, cols] + (1.0 - BETA) * outer
                stats[i, rows, cols] = now
                total = total + jnp.sum(now * now)
                ah[i, rows, cols], al[i, rows, cols] = split(now)
            stores[i].start()
            scale.append(2.5 / jnp.sqrt(total + 1e-06))
            scale_sq.append(6.25 / (total + 1e-06))

        def quarters(corner, wide):
            return (low, low, corner), (low, high, wide[low]), (high, high, wide[high])

        def mirror(i, *refs):
            for ref in refs:
                ref[i, high, low] = ref[i, low, high].T

        for i in range(2):
            a = (ah[i], al[i])
            q00, q01, q11 = square(a, a, low, high)
            for rows, cols, outer in ((low, low, q00), (low, high, q01), (high, high, q11)):
                m = scale[i] * stats[i, rows, cols]
                second = jnp.where(scale_sq[i] > 0.0, scale_sq[i] * outer, 0.0)
                dv = second + D[1] * m
                fv = F[2] * second + F[1] * m
                bv = Q * second + BASE_M * m
                if rows == cols:
                    dv = dv + D[0] * eye[...]
                    fv = fv + F[0] * eye[...]
                    bv = bv + BASE_I * eye[...]
                dm[i, rows, cols] = dv.astype(BF16)
                fm[i, rows, cols] = fv.astype(BF16)
                base[i, rows, cols] = bv
            mirror(i, dm, fm)
        for i in range(2):
            wide = dot(dm[i], fm[i, :, high], False)
            corner = dot(dm[i, low, :], fm[i, :, low], False)
            for rows, cols, outer in quarters(corner, wide):
                ev = outer + E_BASE * base[i, rows, cols] + (E_M * scale[i]) * stats[i, rows, cols]
                if rows == cols:
                    ev = ev + E_I * eye[...]
                em[i, rows, cols] = ev.astype(BF16)
            mirror(i, em)
        for i in range(2):
            wide = dot(dm[i], em[i, :, high], False)
            corner = dot(dm[i, low, :], em[i, :, low], False)
            for rows, cols, outer in quarters(corner, wide):
                kh[i, rows, cols], kl[i, rows, cols] = split(outer + base[i, rows, cols])
            mirror(i, kh, kl)
        both = jnp.sqrt(jnp.sqrt(scale[0])) * jnp.sqrt(jnp.sqrt(scale[1]))
        u = split(both * product((kh[0], kl[0]), (g[0], g[1])))
        total = 0.0
        for t in range(2):
            cols = (low, high)[t]
            result = product(u, part((kh[1], kl[1]), ALL, cols))
            total = total + jnp.sum(result * result)
            for d in range(owners):
                for j in range(2):
                    out_ref[pl.ds(d * per + rows_out * (2 * t + j), rows_out), :] = result[
                        d * rows_out : (d + 1) * rows_out, 128 * j : 128 * (j + 1)
                    ]
        write_sums(total)
        for store in stores:
            store.wait()


def gather_kernel(columns, slots_ref, in_ref, out_ref):
    size = out_ref.shape[-1] // columns
    rows = out_ref.shape[1]
    for b in range(slots_ref.shape[0]):
        r, c = divmod(b, columns)
        slot = slots_ref[b]
        for t in range(size // 128):
            out_ref[r, :, pl.ds(c * size + t * 128, 128)] = in_ref[slot, pl.ds(t * rows, rows), 0, :]


def graft_kernel(*refs):
    *sum_refs, in_ref, out_ref, scaled, sem = refs
    total = sum_refs[0][...]
    for ref in sum_refs[1:]:
        total = total + ref[...]
    ratio = jnp.sqrt(total[:, 1:2] / (total[:, 0:1] + 1e-06))
    copies = []
    for r in range(in_ref.shape[0]):
        scaled[r] = in_ref[r] * ratio
        copies.append(pltpu.make_async_copy(scaled.at[r], out_ref.at[r], sem.at[r]))
        copies[-1].start()
    for copy in copies:
        copy.wait()


SMEM = pl.BlockSpec(memory_space=pltpu.SMEM)
VMEM = pl.BlockSpec(memory_space=pltpu.VMEM)
ANY = pl.BlockSpec(memory_space=pl.ANY)


def shards(grads, left_stats, previous_right_statistics, slot_table):
    _, row_blocks, block_rows, local_width = grads.shape
    size = left_stats.shape[-1]
    columns = local_width // size
    owners = lax.axis_size("dp")
    groups = lax.axis_size("mp")
    assigned = slot_table[0]
    local = grads[0]
    outgoing = pl.pallas_call(
        lambda *refs: pack_kernel(columns, *refs),
        out_shape=jax.ShapeDtypeStruct((owners, block_rows, size), F32),
        in_specs=[ANY, ANY],
        out_specs=VMEM,
        scratch_shapes=[
            pltpu.SMEM(assigned.shape, jnp.int32),
            pltpu.VMEM(local.shape, F32),
            pltpu.SemaphoreType.DMA((row_blocks,)),
            pltpu.SemaphoreType.DMA(()),
        ],
    )(assigned, local)
    arrived = lax.all_to_all(outgoing, "dp", split_axis=0, concat_axis=0, tiled=True)
    grad_sq = jnp.sum(local * local).reshape(1, 1)
    held = jnp.any(assigned == lax.axis_index("dp")).astype(jnp.int32).reshape(1, 1)
    stat = jax.ShapeDtypeStruct((size, size), F32)
    per = (block_rows * size) // 128 + 1
    pair = (2, size, size)
    left_new, right_new, sent = pl.pallas_call(
        owner_kernel,
        out_shape=(stat, stat, jax.ShapeDtypeStruct((owners * per, 128), F32)),
        in_specs=[SMEM, SMEM, VMEM, VMEM, VMEM],
        out_specs=(ANY, ANY, VMEM),
        scratch_shapes=[
            pltpu.VMEM(pair, F32),
            pltpu.SemaphoreType.DMA((2,)),
            *[pltpu.VMEM(pair, BF16)] * 9,
            pltpu.VMEM(pair, F32),
            pltpu.VMEM((size // 2, size // 2), F32),
        ],
        compiler_params=pltpu.CompilerParams(vmem_limit_bytes=40 << 20),
        cost_estimate=pl.CostEstimate(
            flops=60 * size**3, bytes_accessed=6 * 4 * size**2, transcendentals=0
        ),
    )(
        held,
        grad_sq,
        arrived.reshape(size, size),
        left_stats[0, 0],
        previous_right_statistics[0, 0],
    )
    returned = lax.all_to_all(
        sent.reshape(owners, per, 1, 128), "dp", split_axis=0, concat_axis=0, tiled=True
    )
    sums = jnp.sum(returned[:, per - 1, :, :], axis=0)
    others = [
        lax.ppermute(sums, "mp", [(i, (i + k) % groups) for i in range(groups)])
        for k in range(groups - 1, 0, -1)
    ]
    gathered = pl.pallas_call(
        lambda *refs: gather_kernel(columns, *refs),
        out_shape=jax.ShapeDtypeStruct(local.shape, F32),
        in_specs=[SMEM, VMEM],
        out_specs=VMEM,
        compiler_params=pltpu.CompilerParams(vmem_limit_bytes=16 << 20),
        cost_estimate=pl.CostEstimate(flops=0, bytes_accessed=8 << 20, transcendentals=0),
    )(assigned, returned)
    update = pl.pallas_call(
        graft_kernel,
        out_shape=jax.ShapeDtypeStruct(local.shape, F32),
        in_specs=[VMEM] * (groups + 1),
        out_specs=ANY,
        scratch_shapes=[
            pltpu.VMEM(local.shape, F32),
            pltpu.SemaphoreType.DMA((row_blocks,)),
        ],
        compiler_params=pltpu.CompilerParams(vmem_limit_bytes=16 << 20),
    )(sums, *others, gathered)
    return (update[None], left_new[None, None], right_new[None, None])


def solution(mesh):
    return jax.shard_map(
        shards,
        mesh=mesh,
        in_specs=(
            P(None, None, "dp", "mp"),
            P("mp", "dp", None, None),
            P("mp", "dp", None, None),
            P("mp", None),
        ),
        out_specs=(P(None, None, "dp", "mp"), P("mp", "dp", None, None), P("mp", "dp", None, None)),
        check_vma=False,
    )
```

```python
import jax
import jax.numpy as jnp
import numpy as np
from jax import lax
from jax.experimental import pallas as pl
from jax.experimental.pallas import tpu as pltpu
from jax.sharding import PartitionSpec as P

BETA = 0.9
F32 = jnp.float32
BF16 = jnp.bfloat16


poly = np.polynomial.polynomial


def root_plan(first, second, third):
    t = np.array([1.25, -0.25])
    p = poly.polysub(1.25 * t, poly.polymul([0.0, 0.25], poly.polypow(t, 5)))
    d = np.array([first * second, -(first + second), 1.0])
    e, r = poly.polydiv(p, d)
    q = poly.polyval(third, e)
    e = poly.polysub(e, [q])
    f, b = poly.polydiv(e, d)
    s = poly.polyval(third, f)
    f = poly.polysub(f, [s])
    floats = [[float(x) for x in values] for values in (d, r, f, b)]
    return (*floats, float(q), float(s))


D, R, F, B, Q, S = root_plan(0.167, 2.333, 1.25)
BASE_M, BASE_I = Q * D[1] + R[1], Q * D[0] + R[0]
E_BASE = S / Q
E_M, E_I = S * D[1] + B[1] - E_BASE * BASE_M, S * D[0] + B[0] - E_BASE * BASE_I
ALL = slice(None)


def split(x):
    high = x.astype(BF16)
    return high, (x - high.astype(F32)).astype(BF16)


def dot(a, b, transposed):
    dims = (((1,), (1 if transposed else 0,)), ((), ()))
    return lax.dot_general(a, b, dims, preferred_element_type=F32)


def product(a, b, transposed=False):
    (ah, al), (bh, bl) = a, b
    return dot(ah, bh, transposed) + (dot(ah, bl, transposed) + dot(al, bh, transposed))


def square(a, b, low, high, transposed=False):
    (ah, _), (bh, bl) = a, b
    wide = dot(ah, bh[high, :] if transposed else bh[:, high], transposed)
    corner = dot(ah[low], bh[low, :] if transposed else bh[:, low], transposed)
    cross = dot(ah, bl, transposed)
    return (
        corner + (cross[low, low] + cross[low, low].T),
        wide[low] + (cross[low, high] + cross[high, low].T),
        wide[high] + (cross[high, high] + cross[high, high].T),
    )


def part(pair, rows, cols):
    return pair[0][rows, cols], pair[1][rows, cols]


def pack_kernel(columns, slots_hbm, grads_ref, out_ref, slots_ref, held, sem, slots_sem):
    size = out_ref.shape[-1]
    row_blocks = grads_ref.shape[0]
    loads = [
        pltpu.make_async_copy(grads_ref.at[r], held.at[r], sem.at[r]) for r in range(row_blocks)
    ]
    fetch = pltpu.make_async_copy(slots_hbm, slots_ref, slots_sem)
    fetch.start()
    for load in loads:
        load.start()
    fetch.wait()
    for r in range(row_blocks):
        loads[r].wait()
        for c in range(columns):
            out_ref[slots_ref[r * columns + c]] = held[r, :, pl.ds(c * size, size)]


def owner_kernel(
    held_ref, grad_sq_ref, block_ref, left_ref, right_ref,
    new_left_ref, new_right_ref, out_ref,
    stats, sem, g, gt, ah, al, dm, fm, em, kh, kl, base, eye,
):
    size = block_ref.shape[0]
    half = size // 2
    low, high = slice(0, half), slice(half, size)
    previous = [left_ref, right_ref]
    owners = 64
    per = out_ref.shape[0] // owners
    rows_out = size // owners
    grad_sq = grad_sq_ref[0, 0]
    held = held_ref[0, 0] > 0
    stores = [
        pltpu.make_async_copy(stats.at[i], target, sem.at[i])
        for i, target in enumerate([new_left_ref, new_right_ref])
    ]
    lane = lax.broadcasted_iota(jnp.int32, (1, 128), 1)

    def write_sums(prec_sq):
        row = jnp.where(lane == 0, prec_sq, jnp.where(lane == 1, grad_sq, 0.0))
        for d in range(owners):
            out_ref[pl.ds(d * per + per - 1, 1), :] = row

    @pl.when(jnp.logical_not(held))
    def _():
        for i in range(2):
            stats[i] = BETA * previous[i][...]
            stores[i].start()
        write_sums(0.0)
        for store in stores:
            store.wait()

    @pl.when(held)
    def _():
        g[0], g[1] = split(block_ref[...])
        gt[...] = g[0].T
        eye[...] = (
            lax.broadcasted_iota(jnp.int32, (half, half), 0)
            == lax.broadcasted_iota(jnp.int32, (half, half), 1)
        ).astype(F32)
        whole = (g[0], g[1])
        flipped = (gt[...], None)
        scale, scale_sq = [], []
        for i in range(2):
            if i == 0:
                q00, q01, q11 = square(whole, whole, low, high, True)
            else:
                q00, q01, q11 = square(flipped, whole, low, high)
            total = 0.0
            for rows, cols, outer in (
                (low, low, q00),
                (low, high, q01),
                (high, high, q11),
                (high, low, q01.T),
            ):
                now = BETA * previous[i][rows, cols] + (1.0 - BETA) * outer
                stats[i, rows, cols] = now
                total = total + jnp.sum(now * now)
                ah[i, rows, cols], al[i, rows, cols] = split(now)
            stores[i].start()
            scale.append(2.5 / jnp.sqrt(total + 1e-06))
            scale_sq.append(6.25 / (total + 1e-06))

        def quarters(corner, wide):
            return (low, low, corner), (low, high, wide[low]), (high, high, wide[high])

        def mirror(i, *refs):
            for ref in refs:
                ref[i, high, low] = ref[i, low, high].T

        for i in range(2):
            a = (ah[i], al[i])
            q00, q01, q11 = square(a, a, low, high)
            for rows, cols, outer in ((low, low, q00), (low, high, q01), (high, high, q11)):
                m = scale[i] * stats[i, rows, cols]
                second = jnp.where(scale_sq[i] > 0.0, scale_sq[i] * outer, 0.0)
                dv = second + D[1] * m
                fv = F[2] * second + F[1] * m
                bv = Q * second + BASE_M * m
                if rows == cols:
                    dv = dv + D[0] * eye[...]
                    fv = fv + F[0] * eye[...]
                    bv = bv + BASE_I * eye[...]
                dm[i, rows, cols] = dv.astype(BF16)
                fm[i, rows, cols] = fv.astype(BF16)
                base[i, rows, cols] = bv
            mirror(i, dm, fm)
        for i in range(2):
            wide = dot(dm[i], fm[i, :, high], False)
            corner = dot(dm[i, low, :], fm[i, :, low], False)
            for rows, cols, outer in quarters(corner, wide):
                ev = outer + E_BASE * base[i, rows, cols] + (E_M * scale[i]) * stats[i, rows, cols]
                if rows == cols:
                    ev = ev + E_I * eye[...]
                em[i, rows, cols] = ev.astype(BF16)
            mirror(i, em)
        for i in range(2):
            wide = dot(dm[i], em[i, :, high], False)
            corner = dot(dm[i, low, :], em[i, :, low], False)
            for rows, cols, outer in quarters(corner, wide):
                kh[i, rows, cols], kl[i, rows, cols] = split(outer + base[i, rows, cols])
            mirror(i, kh, kl)
        both = jnp.sqrt(jnp.sqrt(scale[0])) * jnp.sqrt(jnp.sqrt(scale[1]))
        u = split(both * product((kh[0], kl[0]), (g[0], g[1])))
        total = 0.0
        for t in range(2):
            cols = (low, high)[t]
            result = product(u, part((kh[1], kl[1]), ALL, cols))
            total = total + jnp.sum(result * result)
            for d in range(owners):
                for j in range(2):
                    out_ref[pl.ds(d * per + rows_out * (2 * t + j), rows_out), :] = result[
                        d * rows_out : (d + 1) * rows_out, 128 * j : 128 * (j + 1)
                    ]
        write_sums(total)
        for store in stores:
            store.wait()


def gather_kernel(columns, slots_ref, in_ref, out_ref):
    size = out_ref.shape[-1] // columns
    rows = out_ref.shape[1]
    for b in range(slots_ref.shape[0]):
        r, c = divmod(b, columns)
        slot = slots_ref[b]
        for t in range(size // 128):
            out_ref[r, :, pl.ds(c * size + t * 128, 128)] = in_ref[slot, pl.ds(t * rows, rows), 0, :]


def graft_kernel(*refs):
    *sum_refs, in_ref, out_ref, scaled, sem = refs
    total = sum_refs[0][...]
    for ref in sum_refs[1:]:
        total = total + ref[...]
    ratio = jnp.sqrt(total[:, 1:2] / (total[:, 0:1] + 1e-06))
    copies = []
    for r in range(in_ref.shape[0]):
        scaled[r] = in_ref[r] * ratio
        copies.append(pltpu.make_async_copy(scaled.at[r], out_ref.at[r], sem.at[r]))
        copies[-1].start()
    for copy in copies:
        copy.wait()


SMEM = pl.BlockSpec(memory_space=pltpu.SMEM)
VMEM = pl.BlockSpec(memory_space=pltpu.VMEM)
ANY = pl.BlockSpec(memory_space=pl.ANY)


def shards(grads, left_stats, previous_right_statistics, slot_table):
    _, row_blocks, block_rows, local_width = grads.shape
    size = left_stats.shape[-1]
    columns = local_width // size
    owners = lax.axis_size("dp")
    groups = lax.axis_size("mp")
    assigned = slot_table[0]
    local = grads[0]
    outgoing = pl.pallas_call(
        lambda *refs: pack_kernel(columns, *refs),
        out_shape=jax.ShapeDtypeStruct((owners, block_rows, size), F32),
        in_specs=[ANY, ANY],
        out_specs=VMEM,
        scratch_shapes=[
            pltpu.SMEM(assigned.shape, jnp.int32),
            pltpu.VMEM(local.shape, F32),
            pltpu.SemaphoreType.DMA((row_blocks,)),
            pltpu.SemaphoreType.DMA(()),
        ],
    )(assigned, local)
    arrived = lax.all_to_all(outgoing, "dp", split_axis=0, concat_axis=0, tiled=True)
    grad_sq = jnp.sum(local * local).reshape(1, 1)
    held = jnp.any(assigned == lax.axis_index("dp")).astype(jnp.int32).reshape(1, 1)
    stat = jax.ShapeDtypeStruct((size, size), F32)
    per = (block_rows * size) // 128 + 1
    pair = (2, size, size)
    left_new, right_new, sent = pl.pallas_call(
        owner_kernel,
        out_shape=(stat, stat, jax.ShapeDtypeStruct((owners * per, 128), F32)),
        in_specs=[SMEM, SMEM, VMEM, VMEM, VMEM],
        out_specs=(ANY, ANY, VMEM),
        scratch_shapes=[
            pltpu.VMEM(pair, F32),
            pltpu.SemaphoreType.DMA((2,)),
            pltpu.VMEM(pair, BF16),
            pltpu.VMEM((size, size), BF16),
            *[pltpu.VMEM(pair, BF16)] * 7,
            pltpu.VMEM(pair, F32),
            pltpu.VMEM((size // 2, size // 2), F32),
        ],
        compiler_params=pltpu.CompilerParams(vmem_limit_bytes=40 << 20),
        cost_estimate=pl.CostEstimate(
            flops=60 * size**3, bytes_accessed=6 * 4 * size**2, transcendentals=0
        ),
    )(
        held,
        grad_sq,
        arrived.reshape(size, size),
        left_stats[0, 0],
        previous_right_statistics[0, 0],
    )
    returned = lax.all_to_all(
        sent.reshape(owners, per, 1, 128), "dp", split_axis=0, concat_axis=0, tiled=True
    )
    sums = jnp.sum(returned[:, per - 1, :, :], axis=0)
    others = [
        lax.ppermute(sums, "mp", [(i, (i + k) % groups) for i in range(groups)])
        for k in range(groups - 1, 0, -1)
    ]
    gathered = pl.pallas_call(
        lambda *refs: gather_kernel(columns, *refs),
        out_shape=jax.ShapeDtypeStruct(local.shape, F32),
        in_specs=[SMEM, VMEM],
        out_specs=VMEM,
        compiler_params=pltpu.CompilerParams(vmem_limit_bytes=16 << 20),
        cost_estimate=pl.CostEstimate(flops=0, bytes_accessed=8 << 20, transcendentals=0),
    )(assigned, returned)
    update = pl.pallas_call(
        graft_kernel,
        out_shape=jax.ShapeDtypeStruct(local.shape, F32),
        in_specs=[VMEM] * (groups + 1),
        out_specs=ANY,
        scratch_shapes=[
            pltpu.VMEM(local.shape, F32),
            pltpu.SemaphoreType.DMA((row_blocks,)),
        ],
        compiler_params=pltpu.CompilerParams(vmem_limit_bytes=16 << 20),
    )(sums, *others, gathered)
    return (update[None], left_new[None, None], right_new[None, None])


def solution(mesh):
    return jax.shard_map(
        shards,
        mesh=mesh,
        in_specs=(
            P(None, None, "dp", "mp"),
            P("mp", "dp", None, None),
            P("mp", "dp", None, None),
            P("mp", None),
        ),
        out_specs=(P(None, None, "dp", "mp"), P("mp", "dp", None, None), P("mp", "dp", None, None)),
        check_vma=False,
    )
```
